128 devices in a mesh: col: 16 (over y, x), gpt: 8 (over z, core).
Axes of the slice: x: 4, y: 4, z: 4, core: 2. Of those that a mesh axis runs over, the one named last changes fastest.
Arguments:
- spectra: bfloat16 [64, 64, 33, 128], P('col', 'gpt'), may hold values from 0.0099487305 to 1
- cloud_top: int32 [64, 64], P('col', 'gpt'), may hold values from 0 to 63
- cloud_depth: int32 [64, 64], P('col', 'gpt'), may hold values from 1 to 64
- sun_order: int32 [64, 64], P('col', 'gpt'), may hold values from -1 to 31, as said below
- sunlit_cos: bfloat16 [64, 64], P('col', 'gpt'), may hold values from 0 to 1, as said below
- albedo: bfloat16 [64, 64, 14], P('col', 'gpt'), may hold values from 0.049804688 to 0.69921875
- temp: float32 [64, 64, 128], P('col', 'gpt'), may hold values from -6 to 6
- extinction: bfloat16 [33, 112], replicated, may hold values from 0.00029945374 to 0.0059814453
- scatter_albedo: float32 [33, 112], replicated, may hold values from 0.5 to 0.95
- gas_depth: float32 [112, 128], replicated, may hold values from 0.0005 to 0.01
- band_map: int32 [112], replicated, may hold values from 0 to 13, never falling along the last dimension, each value on 1 to 16 neighbouring positions
- solar_band: float32 [14], replicated, may hold values from 0.5 to 2
- heat_factor: float32 [128], replicated, may hold values from 1 to 10
Outputs:
- heating: float32 [64, 64, 128], P('col', 'gpt')
- temp_next: float32 [64, 64, 128], P('col', 'gpt')
The draws below stay inside these ranges and needn't reach their ends.
Inputs may be any that keep to these rules, and one draw needn't show every extreme that they name: `sun_order`: every block of 4 x 8 columns of one device is wholly sunlit or wholly dark; a sunlit block carries each rank 0 to 31 once, a dark one -1 everywhere; in every row of such blocks along longitude exactly half are sunlit. `sunlit_cos`: positive exactly at the columns where sun_order is not -1, 0 at the others. `band_map`: never falls along the g-points; each band holds 1 to 2 * 112 // 14 g-points.
All inputs are finite; a program needn't handle non-finite values.
Results may differ from the reference program's by a relative error of at most 0.00056.
Values may be sent and summed in bfloat16 or wider, within the bound.
No kernel may reach another device: no remote copies, remote signals or barrier semaphores. Data moves between devices by JAX's collectives and lax.ppermute only.
A program may use at most 64 MiB of HBM per device.

```python
import math
import jax
import jax.numpy as jnp
import numpy as np
from jax import lax

CLON = 4
CLAT = 8
LEV = 128
BIN = 33
G = 112
NBAND = 14
TILE_COLS = 32
LON = 64
LAT = 64
N_COL = 16
N_GPT = 8


def day_layout(key):
    tile_cols = CLON * CLAT
    offsets = jax.random.randint(jax.random.fold_in(key, 101), (N_GPT,), 0, N_COL)
    tiles_lon = jnp.arange(N_COL, dtype=jnp.int32)
    daylit = (tiles_lon[:, None] - offsets[None, :]) % N_COL < N_COL // 2
    key_list = jax.random.split(jax.random.fold_in(key, 202), N_COL * N_GPT)

    def one_tile(tile_key):
        return jax.random.permutation(tile_key, tile_cols).astype(jnp.int32)
    rank_table = jax.vmap(one_tile)(key_list)
    rank_table = rank_table.reshape(N_COL, N_GPT, CLON, CLAT).transpose(0, 2, 1, 3).reshape(N_COL * CLON, N_GPT * CLAT)
    daylit_cols = jnp.repeat(jnp.repeat(daylit, CLON, axis=0), CLAT, axis=1)
    return (daylit_cols, rank_table)


def draw_sun_order(key, part):
    daylit_cols, rank_table = day_layout(key)
    return jnp.where(daylit_cols, rank_table, -1).astype(jnp.int32)


def draw_sunlit_cos(key, part):
    daylit_cols, rank_table = day_layout(key)
    cos_values = jax.random.uniform(jax.random.fold_in(key, 303), (LON, LAT), jnp.float32, 0.1, 1.0)
    return jnp.where(daylit_cols, cos_values, 0.0).astype(jnp.bfloat16)


def set_ends(array, key, smallest, high):
    extent = array.shape
    place = [jax.random.randint(jax.random.fold_in(key, axis), (), 0, extent[axis]) for axis in range(len(extent))]
    array = array.at[tuple(place)].set(smallest)
    longest = extent.index(max(extent))
    place[longest] = (place[longest] + 1) % extent[longest]
    return array.at[tuple(place)].set(high)


def block_levels(rng, shape, cuts, least, top_value):
    factor_of = 1.0
    for axis_at, shards_of in cuts:
        heights = jax.random.uniform(jax.random.fold_in(jax.random.fold_in(rng, 6), axis_at), (shards_of,), jnp.float32, least / len(cuts), top_value / len(cuts))
        factor_of = factor_of * jnp.repeat(jnp.exp(heights), shape[axis_at] // shards_of).reshape((-1,) + (1,) * (len(shape) - 1 - axis_at))
    return factor_of


def split_up(number_of, total, limit, skew):
    loads = [(1 << 20) // math.isqrt(grade ** skew) + 1 for grade in range(2, number_of + 1)]
    rest, holding = total - limit - (number_of - 1), [1] * (number_of - 1)
    while rest > 0:
        candidates = [i for i in range(number_of - 1) if holding[i] < limit]
        pool, remaining = sum([loads[i] for i in candidates]), rest
        for i in candidates:
            extra = min(limit - holding[i], max(1, remaining * loads[i] // pool), rest)
            holding[i] = holding[i] + extra
            rest = rest - extra
    return np.array([limit] + holding)


def uneven(stream_key, amount, total, most, slope):
    if amount == 2:
        one = jax.random.randint(stream_key, (), max(1, total - most), min(most, total - 1) + 1)
        return jnp.stack([one, total - one])
    tallies = jnp.asarray(split_up(amount, total, most, slope), jnp.int32)
    couples = (amount - 1) // 2
    donor, receiver = tallies[1:1 + 2 * couples:2], tallies[2:2 + 2 * couples:2]
    room = jnp.minimum(donor - 1, most - receiver)
    passed = jax.random.randint(jax.random.fold_in(stream_key, 1), (couples,), 0, 1 << 20) % (room + 1)
    tallies = tallies.at[1:1 + 2 * couples:2].set(donor - passed).at[2:2 + 2 * couples:2].set(receiver + passed)
    return tallies[jax.random.permutation(jax.random.fold_in(stream_key, 2), amount)]


def scatter_about(own_key, extent, scale, most, cuts=(), kind=jnp.bfloat16):
    drawn = jax.random.normal(own_key, extent, jnp.float32) * scale
    if len(cuts) > 0:
        drawn = block_levels(own_key, extent, cuts, -0.22, 0.18) * drawn
    return jnp.clip(drawn, min=-most, max=most).astype(kind)


def setup_inputs(seed: int = 0) -> dict:
    arg_keys = jax.random.split(jax.random.key(seed), 14)
    spectra = jnp.clip(jnp.exp(math.log(1.0) - 4.61031033 * jax.random.uniform(arg_keys[0], (LON, LAT, BIN, LEV), jnp.float32) ** block_levels(arg_keys[0], (LON, LAT, BIN, LEV), ((0, 16), (1, 8)), -0.2, 0.2)), 0.0099487305, 1.0).astype(jnp.bfloat16)
    cloud_top = set_ends(jax.random.randint(arg_keys[1], (LON, LAT), 0, LEV // 2), jax.random.fold_in(arg_keys[1], 1), 0, (LEV // 2) - 1).astype(jnp.int32)
    cloud_depth = set_ends(jax.random.randint(arg_keys[2], (LON, LAT), 1, LEV // 2 + 1), jax.random.fold_in(arg_keys[2], 1), 1, (LEV // 2 + 1) - 1).astype(jnp.int32)
    sun_order = draw_sun_order(jax.random.fold_in(arg_keys[13], 71), 0)
    sunlit_cos = draw_sunlit_cos(jax.random.fold_in(arg_keys[13], 71), 0)
    albedo = jnp.clip(0.049804688 + 0.64941406 * jax.random.uniform(arg_keys[5], (LON, LAT, NBAND), jnp.float32) ** block_levels(arg_keys[5], (LON, LAT, NBAND), ((0, 16), (1, 8)), -0.2, 0.2), 0.049804688, 0.69921875).astype(jnp.bfloat16)
    temp = scatter_about(arg_keys[6], (LON, LAT, LEV), 1.0, 6.0, ((0, 16), (1, 8)), jnp.float32)
    extinction = jnp.clip(jnp.exp(jax.random.uniform(arg_keys[7], (BIN, G), jnp.float32, math.log(0.00029945374), math.log(0.0059814453))), 0.00029945374, 0.0059814453).astype(jnp.bfloat16)
    scatter_albedo = jnp.clip(jax.random.uniform(arg_keys[8], (BIN, G), jnp.float32, 0.5, 0.95), 0.5, 0.95)
    gas_depth = jnp.clip(jnp.exp(jax.random.uniform(arg_keys[9], (G, LEV), jnp.float32, math.log(0.0005), math.log(0.01))), 0.0005, 0.01)
    band_map = jnp.searchsorted(jnp.cumsum(uneven(arg_keys[10], NBAND, G, 2 * G // NBAND, 0)), jnp.arange(G), side="right").astype(jnp.int32)
    solar_band = jnp.clip(jnp.exp(jax.random.uniform(arg_keys[11], (NBAND,), jnp.float32, math.log(0.5), math.log(2.0))), 0.5, 2.0)
    heat_factor = jnp.clip(jnp.exp(jax.random.uniform(arg_keys[12], (LEV,), jnp.float32, math.log(1.0), math.log(10.0))), 1.0, 10.0)
    return {"spectra": spectra, "cloud_top": cloud_top, "cloud_depth": cloud_depth, "sun_order": sun_order, "sunlit_cos": sunlit_cos, "albedo": albedo, "temp": temp, "extinction": extinction, "scatter_albedo": scatter_albedo, "gas_depth": gas_depth, "band_map": band_map, "solar_band": solar_band, "heat_factor": heat_factor}


ASYMMETRY = 0.85
DIFFUSION = 0.2

def mobius_join(earlier, following):
    upper_left = following[0] * earlier[0] + following[1] * earlier[2]
    upper_right = following[0] * earlier[1] + following[1] * earlier[3]
    lower_left = following[2] * earlier[0] + following[3] * earlier[2]
    lower_right = following[2] * earlier[1] + following[3] * earlier[3]
    scale_sum = jnp.abs(upper_left) + jnp.abs(upper_right) + jnp.abs(lower_left) + jnp.abs(lower_right)
    return (upper_left / scale_sum, upper_right / scale_sum, lower_left / scale_sum, lower_right / scale_sum)

def two_stream(ext_total, cloud_sca):
    scat_ratio = cloud_sca / ext_total
    gamma_one = 2.0 - scat_ratio * (1.0 + ASYMMETRY)
    gamma_two = scat_ratio * (1.0 - ASYMMETRY)
    eigen_val = jnp.sqrt((2.0 - 2.0 * scat_ratio) * (2.0 - 2.0 * ASYMMETRY * scat_ratio))
    layer_decay = jnp.exp(-eigen_val * ext_total)
    decay_sq = layer_decay * layer_decay
    denom_sum = eigen_val + gamma_one + (eigen_val - gamma_one) * decay_sq
    reflect = gamma_two * (1.0 - decay_sq) / denom_sum
    transmit = 2.0 * eigen_val * layer_decay / denom_sum
    return (reflect, transmit)

def column_heating(cloud_ext, cloud_sca, gas_part, surface, incoming):
    ext_total = cloud_ext + gas_part
    reflect, transmit = two_stream(ext_total, cloud_sca)
    matrices = (transmit * transmit - reflect * reflect, reflect, -reflect, jnp.ones_like(reflect))
    flipped = tuple((member[..., ::-1] for member in matrices))
    scanned = lax.associative_scan(mobius_join, flipped, axis=2)
    product = tuple((member[..., ::-1] for member in scanned))
    surface_col = surface[..., None]
    reflect_top = (product[0] * surface_col + product[1]) / (product[2] * surface_col + product[3])
    bottom_edge = jnp.broadcast_to(surface_col, reflect_top[..., :1].shape)
    reflect_below = jnp.concatenate([reflect_top[..., 1:], bottom_edge], axis=2)
    factor = transmit / (1.0 - reflect * reflect_below)
    through = lax.associative_scan(jnp.multiply, factor, axis=2)
    above_flux = jnp.concatenate([jnp.ones_like(through[..., :1]), through[..., :-1]], axis=2)
    absorbed = incoming[..., None] * (above_flux * (1.0 - reflect_top) - through * (1.0 - reflect_below))
    return lax.optimization_barrier(jnp.sum(absorbed, axis=1))

def reference(spectra, cloud_top, cloud_depth, sun_order, sunlit_cos, albedo, temp, extinction, scatter_albedo, gas_depth, band_map, solar_band, heat_factor):
    level_ids = jnp.arange(LEV, dtype=jnp.int32)
    cloud_end = cloud_top + cloud_depth
    cloudy = (level_ids >= cloud_top[..., None]) & (level_ids < cloud_end[..., None])
    masked = spectra * cloudy[:, :, None, :].astype(jnp.bfloat16)
    scatter_table = (extinction.astype(jnp.float32) * scatter_albedo).astype(jnp.bfloat16)
    optic_table = jnp.concatenate([extinction, scatter_table], axis=1).astype(jnp.float32)
    solar_g = solar_band[band_map]
    block_count = LON * LAT // TILE_COLS
    spec_blocks = masked.reshape(block_count, TILE_COLS, BIN, LEV)
    cos_blocks = sunlit_cos.astype(jnp.float32).reshape(block_count, TILE_COLS)
    albedo_blocks = albedo.astype(jnp.float32)[..., band_map].reshape(block_count, TILE_COLS, G)
    lit_blocks = (sun_order >= 0).astype(jnp.float32).reshape(block_count, TILE_COLS)

    def one_block(pieces):
        spec_block, cosine, surface_block, lit_block = pieces
        optics = jnp.einsum('cbl,bk->ckl', spec_block.astype(jnp.float32), optic_table, precision=lax.Precision.HIGHEST)
        optics = lax.optimization_barrier(optics.astype(jnp.bfloat16)).astype(jnp.float32)
        incoming = cosine[:, None] * solar_g[None, :]
        summed = column_heating(optics[:, :G], optics[:, G:], gas_depth, surface_block, incoming)
        return summed * lit_block[:, None]
    summed = lax.map(one_block, (spec_blocks, cos_blocks, albedo_blocks, lit_blocks))
    heating = summed.reshape(LON, LAT, LEV) * heat_factor
    laplace = jnp.roll(temp, 1, axis=0) + jnp.roll(temp, -1, axis=0) + jnp.roll(temp, 1, axis=1) + jnp.roll(temp, -1, axis=1) - 4.0 * temp
    temp_next = temp + DIFFUSION * laplace + heating
    return (heating, temp_next)
```

```python
import functools
import jax
import jax.numpy as jnp
from jax import lax
from jax.experimental import pallas as pl
from jax.experimental.pallas import tpu as pltpu
from jax.sharding import PartitionSpec as P

DIFFUSION = 0.2
CHUNK = 8


def column_of(row, size):
    spread = jnp.broadcast_to(row, (size, size))
    lane = lax.broadcasted_iota(jnp.int32, (size, size), 1)
    sublane = lax.broadcasted_iota(jnp.int32, (size, size), 0)
    return jnp.sum(jnp.where(lane == sublane, spread, jnp.zeros_like(spread)), axis=1, keepdims=True)


def radiation_kernel(
    spec_ref, top_ref, depth_ref, order_ref, cos_ref, albedo_ref, temp_ref,
    ext_ref, scat_ref, gas_ref, band_ref, solar_ref, factor_ref,
    heat_ref, base_ref,
    binned, rows_ref, optics, gas_levels, table, steps,
):
    lon, bins, lat, levels = spec_ref.shape
    gpoints = ext_ref.shape[1]
    bands = albedo_ref.shape[2]
    tall = binned.shape[0] // lat
    wide = 128
    block = CHUNK * lon * lat

    table[...] = jnp.zeros_like(table)
    ext = ext_ref[...]
    table[:bins, :gpoints] = ext
    table[:bins, wide : wide + gpoints] = (ext.astype(jnp.float32) * scat_ref[...]).astype(jnp.bfloat16)
    gas_levels[...] = jnp.zeros_like(gas_levels)
    gas_levels[:, :gpoints] = gas_ref[...].T

    onehot = (
        lax.broadcasted_iota(jnp.int32, (bands, gpoints), 0) == band_ref[...]
    ).astype(jnp.float32)
    solar_g = jnp.dot(
        solar_ref[...], onehot, precision=lax.Precision.HIGHEST, preferred_element_type=jnp.float32
    )

    level_lane = lax.broadcasted_iota(jnp.int32, (lat, levels), 1)
    top_all = top_ref[...].astype(jnp.float32)
    end_all = top_all + depth_ref[...].astype(jnp.float32)
    order_all = order_ref[...].astype(jnp.float32)
    cos_all = cos_ref[...].astype(jnp.float32)

    binned[bins * lat :, :] = jnp.zeros((binned.shape[0] - bins * lat, levels), jnp.float32)
    surface, incoming = [], []
    for i in range(lon):
        top = column_of(top_all[i : i + 1], lat)
        end = column_of(end_all[i : i + 1], lat)
        order = column_of(order_all[i : i + 1], lat)
        cosine = column_of(cos_all[i : i + 1], lat)
        lev = level_lane.astype(jnp.float32)
        cloudy = ((lev >= top) & (lev < end)).astype(jnp.float32)
        for b in range(bins):
            binned[b * lat : (b + 1) * lat, :] = spec_ref[i, b].astype(jnp.float32) * cloudy
        for j in range(lat):
            column = binned[pl.ds(j, tall, stride=lat), :]
            rows_ref[pl.ds(i * lat + j, levels, stride=lon * lat), :tall] = column.T
        surf = jnp.dot(
            albedo_ref[i].astype(jnp.bfloat16), onehot.astype(jnp.bfloat16),
            preferred_element_type=jnp.float32,
        )
        lit = (order >= 0.0).astype(jnp.float32)
        surface.append(jnp.pad(surf, ((0, 0), (0, wide - gpoints))))
        incoming.append(jnp.pad((cosine * lit) * solar_g, ((0, 0), (0, wide - gpoints))))

    def fill(chunk, slot):
        start = pl.multiple_of(chunk * block, block)
        lhs = rows_ref[pl.ds(start, block), :tall].astype(jnp.bfloat16)
        optics[slot] = jnp.dot(lhs, table[...], preferred_element_type=jnp.float32)

    count = levels // CHUNK
    fill(count - 1, (count - 1) % 2)

    def one_chunk(k, carry):
        chunk = count - 1 - k
        slot = lax.rem(chunk, 2)
        fill(jnp.maximum(chunk - 1, 0), 1 - slot)
        state = list(carry)
        for step in reversed(range(CHUNK)):
            gas = gas_levels[pl.ds(chunk * CHUNK + step, 1), :]
            for i in range(lon):
                r = (step * lon + i) * lat
                ext = optics[slot, r : r + lat, :wide].astype(jnp.bfloat16).astype(jnp.float32)
                sca = optics[slot, r : r + lat, wide:].astype(jnp.bfloat16).astype(jnp.float32)
                net, both = state[i]
                total = ext + gas
                a = total - sca
                b = total - 0.85 * sca
                p = a * b
                grow = p * (2.0 + p * (2.0 / 3.0 + p * (4.0 / 45.0)))
                slope = 2.0 + p * (4.0 / 3.0 + p * (4.0 / 15.0 + p * (8.0 / 315.0)))
                d_net = grow * net + (a * slope) * both
                d_both = grow * both + (b * slope) * net
                at = pl.multiple_of((chunk * CHUNK + step) * (lon * lat), lon * lat)
                steps[pl.ds(at + i * lat, lat), :] = d_net
                state[i] = (net + d_net, both + d_both)
        return tuple(state)

    start = tuple((1.0 - s, 1.0 + s) for s in surface)
    final = lax.fori_loop(0, count, one_chunk, start)
    weights = [2.0 * q / (net + both) for q, (net, both) in zip(incoming, final)]

    def sum_chunk(chunk, sums):
        sums = list(sums)
        for step in range(CHUNK):
            level = chunk * CHUNK + step
            at = pl.multiple_of(level * (lon * lat), lon * lat)
            here = level_lane == level
            for i in range(lon):
                part = steps[pl.ds(at + i * lat, lat), :] * weights[i]
                sums[i] = jnp.where(here, jnp.sum(part, axis=1, keepdims=True), sums[i])
        return tuple(sums)

    sums = lax.fori_loop(0, count, sum_chunk, tuple(jnp.zeros((lat, levels), jnp.float32) for _ in range(lon)))
    for i in range(lon):
        heat = sums[i] * factor_ref[...]
        heat_ref[i] = heat
        base_ref[i] = temp_ref[i] + heat


def shards(
    spectra, cloud_top, cloud_depth, sun_order, sunlit_cos, albedo, temp,
    extinction, scatter_albedo, gas_depth, band_map, solar_band, heat_factor,
):
    def shift(x, axis, by):
        n = lax.axis_size(axis)
        return lax.ppermute(x, axis, [(i, (i + by) % n) for i in range(n)])

    west = shift(temp, "col", 1)
    east = shift(temp, "col", -1)
    south = shift(temp, "gpt", 1)
    north = shift(temp, "gpt", -1)
    lon, lat, bins, levels = spectra.shape
    gpoints = extinction.shape[1]
    tall = -(-bins // 8) * 8
    shape = jax.ShapeDtypeStruct((lon, lat, levels), jnp.float32)
    heating, base = pl.pallas_call(
        radiation_kernel,
        out_shape=[shape, shape],
        scratch_shapes=[
            pltpu.VMEM((tall * lat, levels), jnp.float32),
            pltpu.VMEM((levels * lon * lat, 128), jnp.float32),
            pltpu.VMEM((2, CHUNK * lon * lat, 256), jnp.float32),
            pltpu.VMEM((levels, 128), jnp.float32),
            pltpu.VMEM((tall, 256), jnp.bfloat16),
            pltpu.VMEM((levels * lon * lat, 128), jnp.float32),
        ],
        compiler_params=pltpu.CompilerParams(vmem_limit_bytes=32 * 1024 * 1024),
        name="radiation",
    )(
        jnp.transpose(spectra, (0, 2, 1, 3)), cloud_top, cloud_depth, sun_order, sunlit_cos, albedo, temp,
        extinction, scatter_albedo, gas_depth, band_map[None], solar_band[None], heat_factor[None],
    )
    up = jnp.concatenate([west[lon - 1 :], temp[: lon - 1]], axis=0)
    down = jnp.concatenate([temp[1:], east[:1]], axis=0)
    left = jnp.concatenate([south[:, lat - 1 :], temp[:, : lat - 1]], axis=1)
    right = jnp.concatenate([temp[:, 1:], north[:, :1]], axis=1)
    return (heating, base + DIFFUSION * (up + down + left + right - 4.0 * temp))


def solution(mesh):
    column = P("col", "gpt")
    deep = P("col", "gpt", None)
    in_specs = (P("col", "gpt", None, None), column, column, column, column, deep, deep) + (P(),) * 6
    return jax.shard_map(shards, mesh=mesh, in_specs=in_specs, out_specs=(deep, deep), check_vma=False)
```

```python
import functools
import jax
import jax.numpy as jnp
from jax import lax
from jax.experimental import pallas as pl
from jax.experimental.pallas import tpu as pltpu
from jax.sharding import PartitionSpec as P

DIFFUSION = 0.2
CHUNK = 8
SUM_CHUNK = 32


def column_of(row, size):
    spread = jnp.broadcast_to(row, (size, size))
    lane = lax.broadcasted_iota(jnp.int32, (size, size), 1)
    sublane = lax.broadcasted_iota(jnp.int32, (size, size), 0)
    return jnp.sum(jnp.where(lane == sublane, spread, jnp.zeros_like(spread)), axis=1, keepdims=True)


def radiate(
    spec_ref, top_ref, depth_ref, order_ref, cos_ref, albedo_ref,
    ext_ref, scat_ref, gas_ref, band_ref, solar_ref, factor_ref,
    heat_ref,
    binned, rows_ref, optics, gas_levels, table, steps,
):
    lon, bins, lat, levels = spec_ref.shape
    gpoints = ext_ref.shape[1]
    bands = albedo_ref.shape[2]
    tall = binned.shape[0] // lat
    wide = 128
    block = CHUNK * lon * lat

    table[...] = jnp.zeros_like(table)
    ext = ext_ref[...]
    table[:bins, :gpoints] = ext
    table[:bins, wide : wide + gpoints] = (ext.astype(jnp.float32) * scat_ref[...]).astype(jnp.bfloat16)
    gas_levels[...] = jnp.zeros_like(gas_levels)
    gas_levels[:, :gpoints] = gas_ref[...].T

    onehot = (
        lax.broadcasted_iota(jnp.int32, (bands, gpoints), 0) == band_ref[...]
    ).astype(jnp.float32)
    solar_g = jnp.dot(
        solar_ref[...], onehot, precision=lax.Precision.HIGHEST, preferred_element_type=jnp.float32
    )

    level_lane = lax.broadcasted_iota(jnp.int32, (lat, levels), 1)
    top_all = top_ref[...].astype(jnp.float32)
    end_all = top_all + depth_ref[...].astype(jnp.float32)
    order_all = order_ref[...].astype(jnp.float32)
    cos_all = cos_ref[...].astype(jnp.float32)

    binned[bins * lat :, :] = jnp.zeros((binned.shape[0] - bins * lat, levels), jnp.float32)
    surface, incoming = [], []
    for i in range(lon):
        top = column_of(top_all[i : i + 1], lat)
        end = column_of(end_all[i : i + 1], lat)
        order = column_of(order_all[i : i + 1], lat)
        cosine = column_of(cos_all[i : i + 1], lat)
        lev = level_lane.astype(jnp.float32)
        cloudy = ((lev >= top) & (lev < end)).astype(jnp.float32)
        for b in range(bins):
            binned[b * lat : (b + 1) * lat, :] = spec_ref[i, b].astype(jnp.float32) * cloudy
        for j in range(lat):
            column = binned[pl.ds(j, tall, stride=lat), :]
            rows_ref[pl.ds(i * lat + j, levels, stride=lon * lat), :tall] = column.T
        surf = jnp.dot(
            albedo_ref[i].astype(jnp.bfloat16), onehot.astype(jnp.bfloat16),
            preferred_element_type=jnp.float32,
        )
        lit = (order >= 0.0).astype(jnp.float32)
        surface.append(jnp.pad(surf, ((0, 0), (0, wide - gpoints))))
        incoming.append(jnp.pad((cosine * lit) * solar_g, ((0, 0), (0, wide - gpoints))))

    piece = 4 * block
    for start_row in range(0, levels * lon * lat, piece):
        lhs = rows_ref[start_row : start_row + piece, :tall].astype(jnp.bfloat16)
        optics[start_row : start_row + piece, :] = jnp.dot(
            lhs, table[...], preferred_element_type=jnp.float32
        ).astype(jnp.bfloat16)

    count = levels // CHUNK

    def one_chunk(k, carry):
        chunk = count - 1 - k
        state = list(carry)
        for step in reversed(range(CHUNK)):
            gas = gas_levels[pl.ds(chunk * CHUNK + step, 1), :]
            at = pl.multiple_of((chunk * CHUNK + step) * (lon * lat), lon * lat)
            ext_two = [optics[pl.ds(at + 2 * i * lat, 2 * lat), :wide].astype(jnp.float32) for i in range(lon // 2)]
            sca_two = [optics[pl.ds(at + 2 * i * lat, 2 * lat), wide:].astype(jnp.float32) for i in range(lon // 2)]
            for i in range(lon):
                half = slice((i % 2) * lat, (i % 2 + 1) * lat)
                ext = ext_two[i // 2][half]
                sca = sca_two[i // 2][half]
                net, both = state[i]
                total = ext + gas
                a = total - sca
                b = total - 0.85 * sca
                p = a * b
                grow = p * (2.0 + p * (2.0 / 3.0 + p * (4.0 / 45.0)))
                slope = 2.0 + p * (4.0 / 3.0 + p * (4.0 / 15.0 + p * (8.0 / 315.0)))
                d_net = grow * net + (a * slope) * both
                d_both = grow * both + (b * slope) * net
                steps[pl.ds(at + i * lat, lat), :] = d_net
                state[i] = (net + d_net, both + d_both)
        return tuple(state)

    start = tuple((1.0 - s, 1.0 + s) for s in surface)
    final = lax.fori_loop(0, count, one_chunk, start)
    weights = [2.0 * q / (net + both) for q, (net, both) in zip(incoming, final)]

    def sum_chunk(chunk, sums):
        sums = list(sums)
        for step in range(SUM_CHUNK):
            level = chunk * SUM_CHUNK + step
            at = pl.multiple_of(level * (lon * lat), lon * lat)
            here = level_lane == level
            for i in range(lon):
                part = steps[pl.ds(at + i * lat, lat), :] * weights[i]
                sums[i] = jnp.where(here, jnp.sum(part, axis=1, keepdims=True), sums[i])
        return tuple(sums)

    sums = lax.fori_loop(0, levels // SUM_CHUNK, sum_chunk, tuple(jnp.zeros((lat, levels), jnp.float32) for _ in range(lon)))
    for i in range(lon):
        heat_ref[i] = sums[i] * factor_ref[...]


def radiation_kernel(*refs):
    count = 13
    sources, heat_ref, base_ref = refs[:count], refs[count], refs[count + 1]
    held, scratch, arrived = refs[count + 2 : 2 * count + 2], refs[2 * count + 2 : -1], refs[-1]
    copies = [pltpu.make_async_copy(s, h, arrived.at[n]) for n, (s, h) in enumerate(zip(sources, held))]
    for copy in copies:
        copy.start()
    for copy in copies:
        copy.wait()
    radiate(*held[:-1], heat_ref, *scratch)
    temp_ref = held[-1]
    lon, lat, levels = temp_ref.shape
    edge = jnp.zeros((1, levels), jnp.float32)
    for i in range(lon):
        here = temp_ref[i]
        around = jnp.concatenate([edge, here[: lat - 1]], axis=0) + jnp.concatenate([here[1:], edge], axis=0)
        if i > 0:
            around += temp_ref[i - 1]
        if i < lon - 1:
            around += temp_ref[i + 1]
        base_ref[i] = here + DIFFUSION * (around - 4.0 * here) + heat_ref[i]


def shards(
    spectra, cloud_top, cloud_depth, sun_order, sunlit_cos, albedo, temp,
    extinction, scatter_albedo, gas_depth, band_map, solar_band, heat_factor,
):
    def swap(axis, odd):
        n = lax.axis_size(axis)
        partner = [(i ^ 1) if odd == 0 else ((i + 1) % n if i % 2 else (i - 1) % n) for i in range(n)]
        return lax.ppermute(temp, axis, list(enumerate(partner)))

    col_a, col_b, gpt_a, gpt_b = swap("col", 0), swap("col", 1), swap("gpt", 0), swap("gpt", 1)
    lon, lat, bins, levels = spectra.shape
    tall = -(-bins // 8) * 8
    shape = jax.ShapeDtypeStruct((lon, lat, levels), jnp.float32)
    inputs = (
        jnp.transpose(spectra, (0, 2, 1, 3)), cloud_top, cloud_depth, sun_order, sunlit_cos, albedo,
        extinction, scatter_albedo, gas_depth, band_map[None], solar_band[None], heat_factor[None], temp,
    )
    heating, base = pl.pallas_call(
        radiation_kernel,
        out_shape=[shape, shape],
        in_specs=[pl.BlockSpec(memory_space=pltpu.HBM)] * len(inputs),
        scratch_shapes=[pltpu.VMEM(x.shape, x.dtype) for x in inputs]
        + [
            pltpu.VMEM((tall * lat, levels), jnp.float32),
            pltpu.VMEM((levels * lon * lat, 128), jnp.float32),
            pltpu.VMEM((levels * lon * lat, 256), jnp.bfloat16),
            pltpu.VMEM((levels, 128), jnp.float32),
            pltpu.VMEM((tall, 256), jnp.bfloat16),
            pltpu.VMEM((levels * lon * lat, 128), jnp.float32),
            pltpu.SemaphoreType.DMA((len(inputs),)),
        ],
        compiler_params=pltpu.CompilerParams(vmem_limit_bytes=60 * 1024 * 1024),
        cost_estimate=pl.CostEstimate(flops=200_000_000, bytes_accessed=1 << 20, transcendentals=0),
        name="radiation",
    )(*inputs)
    col_a, col_b, gpt_a, gpt_b, base = lax.optimization_barrier((col_a, col_b, gpt_a, gpt_b, base))
    col_even = lax.rem(lax.axis_index("col"), 2) == 0
    gpt_even = lax.rem(lax.axis_index("gpt"), 2) == 0
    west = jnp.where(col_even, col_b[lon - 1 :], col_a[lon - 1 :])
    east = jnp.where(col_even, col_a[:1], col_b[:1])
    south = jnp.where(gpt_even, gpt_b[:, lat - 1 :], gpt_a[:, lat - 1 :])
    north = jnp.where(gpt_even, gpt_a[:, :1], gpt_b[:, :1])
    temp_next = base + DIFFUSION * (
        jnp.pad(west, ((0, lon - 1), (0, 0), (0, 0)))
        + jnp.pad(east, ((lon - 1, 0), (0, 0), (0, 0)))
        + jnp.pad(south, ((0, 0), (0, lat - 1), (0, 0)))
        + jnp.pad(north, ((0, 0), (lat - 1, 0), (0, 0)))
    )
    return (heating, temp_next)


def solution(mesh):
    column = P("col", "gpt")
    deep = P("col", "gpt", None)
    in_specs = (P("col", "gpt", None, None), column, column, column, column, deep, deep) + (P(),) * 6
    return jax.shard_map(shards, mesh=mesh, in_specs=in_specs, out_specs=(deep, deep), check_vma=False)
```

```python
import jax
import jax.numpy as jnp
from jax import lax
from jax.experimental import pallas as pl
from jax.experimental.pallas import tpu as pltpu
from jax.sharding import PartitionSpec as P

DIFFUSION = 0.2
CHUNK = 8
PAIR = 2
INPUTS = 13
WIDE = 128


def column_of(row, size):
    spread = jnp.broadcast_to(row, (size, size))
    lane = lax.broadcasted_iota(jnp.int32, (size, size), 1)
    sublane = lax.broadcasted_iota(jnp.int32, (size, size), 0)
    return jnp.sum(jnp.where(lane == sublane, spread, jnp.zeros_like(spread)), axis=1, keepdims=True)


def radiate(
    first, last,
    spec_ref, top_ref, depth_ref, order_ref, cos_ref, albedo_ref,
    ext_ref, scat_ref, gas_ref, band_ref, solar_ref, factor_ref, top_scalars,
    heat_ref,
    binned, rows_ref, optics, gas_levels, table, steps, flat, gas_window, e_levels, clear_high, clear_low, ends,
):
    lon, bins, lat, levels = spec_ref.shape
    gpoints = ext_ref.shape[1]
    bands = albedo_ref.shape[2]
    tall = binned.shape[0] // lat
    group = PAIR * lat
    window = levels // 2

    table[...] = jnp.zeros_like(table)
    ext = ext_ref[...]
    table[:bins, :gpoints] = ext
    table[:bins, WIDE : WIDE + gpoints] = (ext.astype(jnp.float32) * scat_ref[...]).astype(jnp.bfloat16)

    gas = jnp.pad(gas_ref[...], ((0, WIDE - gpoints), (0, 0)))
    under = lax.broadcasted_iota(jnp.int32, (levels, levels), 0) > lax.broadcasted_iota(jnp.int32, (levels, levels), 1)
    below = jnp.dot(
        gas, under.astype(jnp.float32), precision=lax.Precision.HIGHEST, preferred_element_type=jnp.float32
    )
    t = 2.0 * gas
    rise = t * (1.0 + t * (0.5 + t * (1.0 / 6.0 + t * (1.0 / 24.0))))
    growth_below = jnp.exp(2.0 * below)
    growth = growth_below * (1.0 + rise)
    gas_levels[...] = gas.T
    e_levels[...] = growth.T
    for n, part in enumerate((growth_below * rise, rise / growth)):
        high = part.astype(jnp.bfloat16)
        clear_high[n * WIDE : (n + 1) * WIDE, :] = high
        clear_low[n * WIDE : (n + 1) * WIDE, :] = (part - high.astype(jnp.float32)).astype(jnp.bfloat16)

    onehot = (
        lax.broadcasted_iota(jnp.int32, (bands, gpoints), 0) == band_ref[...]
    ).astype(jnp.float32)
    solar_g = jnp.dot(
        solar_ref[...], onehot, precision=lax.Precision.HIGHEST, preferred_element_type=jnp.float32
    )
    onehot = onehot.astype(jnp.bfloat16)
    lev = lax.broadcasted_iota(jnp.int32, (lat, levels), 1).astype(jnp.float32)
    top = top_ref[...].astype(jnp.float32)
    flat[0, :lon, :lat] = top
    flat[1, :lon, :lat] = top + depth_ref[...].astype(jnp.float32)
    flat[2, :lon, :lat] = order_ref[...].astype(jnp.float32)
    flat[3, :lon, :lat] = cos_ref[...].astype(jnp.float32)
    binned[bins * lat :, :] = jnp.zeros((binned.shape[0] - bins * lat, levels), jnp.float32)

    def one_pair(pair, nothing):
        surface, incoming, tops = [], [], []
        for i in range(PAIR):
            at_lon = pair * PAIR + i
            top, end, order, cosine = (column_of(flat[n, pl.ds(at_lon, 1), :lat], lat) for n in range(4))
            cloudy = ((lev >= top) & (lev < end)).astype(jnp.float32)
            for b in range(bins):
                binned[b * lat : (b + 1) * lat, :] = spec_ref[at_lon, b].astype(jnp.float32) * cloudy
            for j in range(lat):
                c = i * lat + j
                start = top_scalars[at_lon, j]
                column = pltpu.roll(binned[pl.ds(j, tall, stride=lat), :], lax.rem(levels - start, levels), 1)
                rows_ref[pl.ds(c, window, stride=group), :tall] = column.T[:window]
                gas_window[pl.ds(c, window, stride=group), :] = gas_levels[pl.ds(start, window), :]
                ends[0, c : c + 1, :] = e_levels[pl.ds(start, 1), :]
                ends[1, c : c + 1, :] = e_levels[pl.ds(start + window, 1), :]
            surf = jnp.dot(albedo_ref[at_lon], onehot, preferred_element_type=jnp.float32)
            lit = (order >= 0.0).astype(jnp.float32)
            surface.append(jnp.pad(surf, ((0, 0), (0, WIDE - gpoints))))
            incoming.append(jnp.pad((cosine * lit) * solar_g, ((0, 0), (0, WIDE - gpoints))))
            tops.append(top)

        lhs = rows_ref[:, :tall].astype(jnp.bfloat16)
        optics[...] = jnp.dot(lhs, table[...], preferred_element_type=jnp.float32).astype(jnp.bfloat16)

        def one_chunk(k, carry):
            chunk = window // CHUNK - 1 - k
            state = list(carry)
            for step in reversed(range(CHUNK)):
                at = pl.multiple_of((chunk * CHUNK + step) * group, group)
                ext_pair = optics[pl.ds(at, group), :WIDE].astype(jnp.float32)
                sca_pair = optics[pl.ds(at, group), WIDE:].astype(jnp.float32)
                for i in range(PAIR):
                    ext, sca = ext_pair[i * lat : (i + 1) * lat], sca_pair[i * lat : (i + 1) * lat]
                    net, both = state[i]
                    total = ext + gas_window[pl.ds(at + i * lat, lat), :]
                    a = total - sca
                    b = total - 0.85 * sca
                    p = a * b
                    grow = p * (2.0 + p * (2.0 / 3.0 + p * (4.0 / 45.0)))
                    slope = 2.0 + p * (4.0 / 3.0 + p * (4.0 / 15.0 + p * (8.0 / 315.0)))
                    d_net = grow * net + (a * slope) * both
                    d_both = grow * both + (b * slope) * net
                    steps[pl.ds(at + i * lat, lat), :] = d_net
                    state[i] = (net + d_net, both + d_both)
            return tuple(state)

        begin = []
        for i in range(PAIR):
            e_end = ends[1, i * lat : (i + 1) * lat, :]
            upward = surface[i] / e_end
            begin.append((e_end - upward, e_end + upward))
        final = lax.fori_loop(0, window // CHUNK, one_chunk, tuple(begin))

        weights, clear = [], []
        for i, (net, both) in enumerate(final):
            e_top = ends[0, i * lat : (i + 1) * lat, :]
            over = incoming[i] / e_levels[:1, :]
            weight = 2.0 * over * e_top / (net + both)
            weights.append(weight)
            clear.append(jnp.concatenate([over, 0.5 * weight * (both - net) * e_top], axis=1))
            clear.append(jnp.concatenate([weight, weight * surface[i]], axis=1))
        clear = jnp.concatenate(clear, axis=0)
        high = clear.astype(jnp.bfloat16)
        low = (clear - high.astype(jnp.float32)).astype(jnp.bfloat16)
        outside = (
            jnp.dot(high, clear_high[...], preferred_element_type=jnp.float32)
            + jnp.dot(high, clear_low[...], preferred_element_type=jnp.float32)
            + jnp.dot(low, clear_high[...], preferred_element_type=jnp.float32)
        )

        for i in range(PAIR):
            place = lev - tops[i]
            sums = jnp.where(place < 0.0, outside[2 * i * lat : (2 * i + 1) * lat],
                             outside[(2 * i + 1) * lat : (2 * i + 2) * lat])
            for k in range(window):
                part = steps[k * group + i * lat : k * group + (i + 1) * lat, :] * weights[i]
                sums = jnp.where(place == float(k), jnp.sum(part, axis=1, keepdims=True), sums)
            heat_ref[pair * PAIR + i] = sums * factor_ref[...]
        return nothing

    lax.fori_loop(first, last, one_pair, 0)


def pairs_ahead():
    at_col, at_gpt = lax.axis_index("col"), lax.axis_index("gpt")
    y, x, z = at_col // 4, lax.rem(at_col, 4), at_gpt // 2
    place = 8 * x + 9 * y + 13 * z
    return jnp.where(place <= -1, 2, jnp.where(place <= 30, 1, 0))


def fetch(sources, held, arrived):
    copies = [pltpu.make_async_copy(s, h, arrived.at[n]) for n, (s, h) in enumerate(zip(sources, held))]
    for copy in copies:
        copy.start()
    for copy in copies:
        copy.wait()


def ahead_kernel(*refs):
    count = INPUTS
    sources, out_ref = refs[:count], refs[count]
    held, heat_ref = refs[count + 1 : 2 * count + 1], refs[2 * count + 1]
    scratch, arrived = refs[2 * count + 2 : -1], refs[-1]
    pairs = pairs_ahead()

    @pl.when(pairs > 0)
    def _():
        fetch(sources, held, arrived)
        radiate(0, pairs, *held, heat_ref, *scratch)
        leave = pltpu.make_async_copy(heat_ref, out_ref, arrived.at[0])
        leave.start()
        leave.wait()


def after_kernel(temp_ref, early_ref, *refs):
    count = INPUTS
    sources, (heat_ref, base_ref) = refs[:count], refs[count : count + 2]
    held, scratch = refs[count + 2 : 2 * count + 2], refs[2 * count + 2 : -3]
    own_ref, two, arrived = refs[-3:]
    lon, lat, levels = temp_ref.shape
    pairs = pairs_ahead()
    early = pltpu.make_async_copy(early_ref, heat_ref, two.at[0])
    early.start()
    own = pltpu.make_async_copy(temp_ref, own_ref, two.at[1])
    own.start()

    @pl.when(pairs < lon // PAIR)
    def _():
        fetch(sources, held, arrived)

    early.wait()
    own.wait()
    temp_ref = own_ref

    @pl.when(pairs < lon // PAIR)
    def _():
        radiate(pairs, lon // PAIR, *held, heat_ref, *scratch)

    edge = jnp.zeros((1, levels), jnp.float32)
    for i in range(lon):
        here = temp_ref[i]
        around = jnp.concatenate([edge, here[: lat - 1]], axis=0) + jnp.concatenate([here[1:], edge], axis=0)
        if i > 0:
            around += temp_ref[i - 1]
        if i < lon - 1:
            around += temp_ref[i + 1]
        base_ref[i] = here + DIFFUSION * (around - 4.0 * here) + heat_ref[i]


def shards(
    spectra, cloud_top, cloud_depth, sun_order, sunlit_cos, albedo, temp,
    extinction, scatter_albedo, gas_depth, band_map, solar_band, heat_factor,
):
    lon, lat, bins, levels = spectra.shape
    tall = -(-bins // 8) * 8
    rows = levels // 2 * PAIR * lat
    shape = jax.ShapeDtypeStruct((lon, lat, levels), jnp.float32)
    inputs = (
        jnp.transpose(spectra, (0, 2, 1, 3)), cloud_top, cloud_depth, sun_order, sunlit_cos, albedo,
        extinction, scatter_albedo, gas_depth, band_map[None], solar_band[None], heat_factor[None],
        cloud_top,
    )
    apart = [pl.BlockSpec(memory_space=pltpu.HBM)] * len(inputs)
    held = [pltpu.VMEM(x.shape, x.dtype) for x in inputs[:-1]] + [pltpu.SMEM(cloud_top.shape, cloud_top.dtype)]
    scratch = [
        pltpu.VMEM((tall * lat, levels), jnp.float32),
        pltpu.VMEM((rows, WIDE), jnp.float32),
        pltpu.VMEM((rows, 2 * WIDE), jnp.bfloat16),
        pltpu.VMEM((levels, WIDE), jnp.float32),
        pltpu.VMEM((tall, 2 * WIDE), jnp.bfloat16),
        pltpu.VMEM((rows, WIDE), jnp.float32),
        pltpu.VMEM((4, 8, WIDE), jnp.float32),
        pltpu.VMEM((rows, WIDE), jnp.float32),
        pltpu.VMEM((levels, WIDE), jnp.float32),
        pltpu.VMEM((2 * WIDE, levels), jnp.bfloat16),
        pltpu.VMEM((2 * WIDE, levels), jnp.bfloat16),
        pltpu.VMEM((2, PAIR * lat, WIDE), jnp.float32),
        pltpu.SemaphoreType.DMA((len(inputs),)),
    ]
    params = pltpu.CompilerParams(vmem_limit_bytes=60 * 1024 * 1024)
    early = pl.pallas_call(
        ahead_kernel,
        out_shape=shape,
        in_specs=apart,
        out_specs=pl.BlockSpec(memory_space=pltpu.HBM),
        scratch_shapes=held + [pltpu.VMEM(shape.shape, shape.dtype)] + scratch,
        compiler_params=params,
        name="radiation_ahead",
    )(*inputs)
    sent, early = lax.optimization_barrier((temp, early))

    def swap(axis, odd):
        n = lax.axis_size(axis)
        partner = [(i ^ 1) if odd == 0 else ((i + 1) % n if i % 2 else (i - 1) % n) for i in range(n)]
        return lax.ppermute(sent, axis, list(enumerate(partner)))

    col_a, col_b, gpt_a, gpt_b = swap("col", 0), swap("col", 1), swap("gpt", 0), swap("gpt", 1)
    heating, base = pl.pallas_call(
        after_kernel,
        out_shape=[shape, shape],
        in_specs=apart[:2] + apart,
        scratch_shapes=held
        + scratch[:-1]
        + [pltpu.VMEM(shape.shape, shape.dtype), pltpu.SemaphoreType.DMA((2,)), scratch[-1]],
        compiler_params=params,
        cost_estimate=pl.CostEstimate(flops=200_000_000, bytes_accessed=1 << 20, transcendentals=0),
        name="radiation_after",
    )(temp, early, *inputs)
    gpt_a, col_b, col_a, gpt_b = lax.optimization_barrier((gpt_a, col_b, col_a, gpt_b))
    base = lax.optimization_barrier(base)
    col_even = lax.rem(lax.axis_index("col"), 2) == 0
    gpt_even = lax.rem(lax.axis_index("gpt"), 2) == 0
    west = jnp.where(col_even, col_b[lon - 1 :], col_a[lon - 1 :])
    east = jnp.where(col_even, col_a[:1], col_b[:1])
    south = jnp.where(gpt_even, gpt_b[:, lat - 1 :], gpt_a[:, lat - 1 :])
    north = jnp.where(gpt_even, gpt_a[:, :1], gpt_b[:, :1])
    temp_next = base + DIFFUSION * (
        jnp.pad(west, ((0, lon - 1), (0, 0), (0, 0)))
        + jnp.pad(east, ((lon - 1, 0), (0, 0), (0, 0)))
        + jnp.pad(south, ((0, 0), (0, lat - 1), (0, 0)))
        + jnp.pad(north, ((0, 0), (lat - 1, 0), (0, 0)))
    )
    return (heating, temp_next)


def solution(mesh):
    column = P("col", "gpt")
    deep = P("col", "gpt", None)
    in_specs = (P("col", "gpt", None, None), column, column, column, column, deep, deep) + (P(),) * 6
    return jax.shard_map(shards, mesh=mesh, in_specs=in_specs, out_specs=(deep, deep), check_vma=False)
```

```python
import jax
import jax.numpy as jnp
from jax import lax
from jax.experimental import pallas as pl
from jax.experimental.pallas import tpu as pltpu
from jax.sharding import PartitionSpec as P

DIFFUSION = 0.2
CHUNK = 8
PAIR = 2
INPUTS = 13
PLAN = (84235610, 1029, 5, 0)
WIDE = 128


def column_of(row, size):
    spread = jnp.broadcast_to(row, (size, size))
    lane = lax.broadcasted_iota(jnp.int32, (size, size), 1)
    sublane = lax.broadcasted_iota(jnp.int32, (size, size), 0)
    return jnp.sum(jnp.where(lane == sublane, spread, jnp.zeros_like(spread)), axis=1, keepdims=True)


def radiate(
    spectra, first, last,
    spec_ref, top_ref, depth_ref, order_ref, cos_ref, albedo_ref,
    ext_ref, scat_ref, gas_ref, band_ref, solar_ref, factor_ref, top_scalars,
    heat_ref,
    binned, rows_ref, gas_levels, table, steps, flat, gas_window, e_levels, clear_high, clear_low, ends,
):
    lon, bins, lat, levels = spec_ref.shape
    gpoints = ext_ref.shape[1]
    bands = albedo_ref.shape[2]
    tall = binned.shape[0] // lat
    group = PAIR * lat
    window = levels // 2

    table[...] = jnp.zeros_like(table)
    ext = ext_ref[...]
    table[:bins, :gpoints] = ext
    table[:bins, WIDE : WIDE + gpoints] = (ext.astype(jnp.float32) * scat_ref[...]).astype(jnp.bfloat16)

    gas = jnp.pad(gas_ref[...], ((0, WIDE - gpoints), (0, 0)))
    under = lax.broadcasted_iota(jnp.int32, (levels, levels), 0) > lax.broadcasted_iota(jnp.int32, (levels, levels), 1)
    below = jnp.dot(
        gas, under.astype(jnp.float32), precision=lax.Precision.HIGHEST, preferred_element_type=jnp.float32
    )
    t = 2.0 * gas
    rise = t * (1.0 + t * (0.5 + t * (1.0 / 6.0 + t * (1.0 / 24.0))))
    growth_below = jnp.exp(2.0 * below)
    growth = growth_below * (1.0 + rise)
    gas_levels[...] = gas.T
    e_levels[...] = growth.T
    for n, part in enumerate((growth_below * rise, rise / growth)):
        high = part.astype(jnp.bfloat16)
        clear_high[n * WIDE : (n + 1) * WIDE, :] = high
        clear_low[n * WIDE : (n + 1) * WIDE, :] = (part - high.astype(jnp.float32)).astype(jnp.bfloat16)

    onehot = (
        lax.broadcasted_iota(jnp.int32, (bands, gpoints), 0) == band_ref[...]
    ).astype(jnp.float32)
    solar_g = jnp.dot(
        solar_ref[...], onehot, precision=lax.Precision.HIGHEST, preferred_element_type=jnp.float32
    )
    onehot = onehot.astype(jnp.bfloat16)
    lev = lax.broadcasted_iota(jnp.int32, (lat, levels), 1).astype(jnp.float32)
    top = top_ref[...].astype(jnp.float32)
    flat[0, :lon, :lat] = top
    flat[1, :lon, :lat] = top + depth_ref[...].astype(jnp.float32)
    flat[2, :lon, :lat] = order_ref[...].astype(jnp.float32)
    flat[3, :lon, :lat] = cos_ref[...].astype(jnp.float32)
    binned[bins * lat :, :] = jnp.zeros((binned.shape[0] - bins * lat, levels), jnp.float32)

    spectra.wait()

    def one_pair(pair, nothing):
        surface, incoming, tops = [], [], []
        for i in range(PAIR):
            at_lon = pair * PAIR + i
            top, end, order, cosine = (column_of(flat[n, pl.ds(at_lon, 1), :lat], lat) for n in range(4))
            cloudy = ((lev >= top) & (lev < end)).astype(jnp.float32)
            for b in range(bins):
                binned[b * lat : (b + 1) * lat, :] = spec_ref[at_lon, b].astype(jnp.float32) * cloudy
            for j in range(lat):
                c = i * lat + j
                start = top_scalars[at_lon, j]
                column = pltpu.roll(binned[pl.ds(j, tall, stride=lat), :], lax.rem(levels - start, levels), 1)
                rows_ref[pl.ds(c, window, stride=group), :tall] = column.T[:window]
                gas_window[pl.ds(c, window, stride=group), :] = gas_levels[pl.ds(start, window), :]
                ends[0, c : c + 1, :] = e_levels[pl.ds(start, 1), :]
                ends[1, c : c + 1, :] = e_levels[pl.ds(start + window, 1), :]
            surf = jnp.dot(albedo_ref[at_lon], onehot, preferred_element_type=jnp.float32)
            lit = (order >= 0.0).astype(jnp.float32)
            surface.append(jnp.pad(surf, ((0, 0), (0, WIDE - gpoints))))
            incoming.append(jnp.pad((cosine * lit) * solar_g, ((0, 0), (0, WIDE - gpoints))))
            tops.append(top)

        begin = []
        for i in range(PAIR):
            e_end = ends[1, i * lat : (i + 1) * lat, :]
            upward = surface[i] / e_end
            begin.append((e_end - upward, e_end + upward))
        state = begin
        part = CHUNK * group
        for chunk in reversed(range(window // CHUNK)):
            lhs = rows_ref[chunk * part : (chunk + 1) * part, :tall].astype(jnp.bfloat16)
            optics = jnp.dot(lhs, table[...], preferred_element_type=jnp.float32).astype(jnp.bfloat16)
            for step in reversed(range(CHUNK)):
                at = (chunk * CHUNK + step) * group
                pair_rows = optics[step * group : (step + 1) * group].astype(jnp.float32)
                for i in range(PAIR):
                    ext = pair_rows[i * lat : (i + 1) * lat, :WIDE]
                    sca = pair_rows[i * lat : (i + 1) * lat, WIDE:]
                    net, both = state[i]
                    total = ext + gas_window[at + i * lat : at + (i + 1) * lat, :]
                    a = total - sca
                    b = total - 0.85 * sca
                    p = a * b
                    grow = p * (2.0 + p * (2.0 / 3.0 + p * (4.0 / 45.0)))
                    slope = 2.0 + p * (4.0 / 3.0 + p * (4.0 / 15.0 + p * (8.0 / 315.0)))
                    d_net = grow * net + (a * slope) * both
                    d_both = grow * both + (b * slope) * net
                    steps[at + i * lat : at + (i + 1) * lat, :] = d_net
                    state[i] = (net + d_net, both + d_both)
        final = state

        weights, clear = [], []
        for i, (net, both) in enumerate(final):
            e_top = ends[0, i * lat : (i + 1) * lat, :]
            over = incoming[i] / e_levels[:1, :]
            weight = 2.0 * over * e_top / (net + both)
            weights.append(weight)
            clear.append(jnp.concatenate([over, 0.5 * weight * (both - net) * e_top], axis=1))
            clear.append(jnp.concatenate([weight, weight * surface[i]], axis=1))
        clear = jnp.concatenate(clear, axis=0)
        high = clear.astype(jnp.bfloat16)
        low = (clear - high.astype(jnp.float32)).astype(jnp.bfloat16)
        outside = (
            jnp.dot(high, clear_high[...], preferred_element_type=jnp.float32)
            + jnp.dot(high, clear_low[...], preferred_element_type=jnp.float32)
            + jnp.dot(low, clear_high[...], preferred_element_type=jnp.float32)
        )

        for i in range(PAIR):
            place = lev - tops[i]
            sums = jnp.where(place < 0.0, outside[2 * i * lat : (2 * i + 1) * lat],
                             outside[(2 * i + 1) * lat : (2 * i + 2) * lat])
            for k in range(window):
                part = steps[k * group + i * lat : k * group + (i + 1) * lat, :] * weights[i]
                sums = jnp.where(place == float(k), jnp.sum(part, axis=1, keepdims=True), sums)
            heat_ref[pair * PAIR + i] = sums * factor_ref[...]
        return nothing

    lax.fori_loop(first, last, one_pair, 0)


def pairs_ahead():
    at_col, at_gpt = lax.axis_index("col"), lax.axis_index("gpt")
    y, x, z = at_col // 4, lax.rem(at_col, 4), at_gpt // 2
    plan = jnp.where(z == 0, PLAN[0], jnp.where(z == 1, PLAN[1], jnp.where(z == 2, PLAN[2], PLAN[3])))
    return lax.shift_right_logical(plan, 2 * at_col) & 3


def fetch(sources, held, arrived):
    copies = [pltpu.make_async_copy(s, h, arrived.at[n]) for n, (s, h) in enumerate(zip(sources, held))]
    for copy in copies:
        copy.start()
    for copy in copies[1:]:
        copy.wait()
    return copies[0]


def ahead_kernel(*refs):
    count = INPUTS
    sources, out_ref = refs[:count], refs[count]
    held, heat_ref = refs[count + 1 : 2 * count + 1], refs[2 * count + 1]
    scratch, arrived = refs[2 * count + 2 : -1], refs[-1]
    pairs = pairs_ahead()

    @pl.when(pairs > 0)
    def _():
        spectra = fetch(sources, held, arrived)
        radiate(spectra, 0, pairs, *held, heat_ref, *scratch)
        leave = pltpu.make_async_copy(heat_ref, out_ref, arrived.at[0])
        leave.start()
        leave.wait()


def after_kernel(temp_ref, early_ref, *refs):
    count = INPUTS
    sources, (heat_ref, base_ref) = refs[:count], refs[count : count + 2]
    held, scratch = refs[count + 2 : 2 * count + 2], refs[2 * count + 2 : -3]
    own_ref, two, arrived = refs[-3:]
    lon, lat, levels = temp_ref.shape
    pairs = pairs_ahead()
    early = pltpu.make_async_copy(early_ref, heat_ref, two.at[0])
    early.start()
    own = pltpu.make_async_copy(temp_ref, own_ref, two.at[1])
    own.start()

    @pl.when(pairs < lon // PAIR)
    def _():
        spectra = fetch(sources, held, arrived)
        early.wait()
        radiate(spectra, pairs, lon // PAIR, *held, heat_ref, *scratch)

    @pl.when(pairs == lon // PAIR)
    def _():
        early.wait()

    own.wait()
    temp_ref = own_ref
    edge = jnp.zeros((1, levels), jnp.float32)
    for i in range(lon):
        here = temp_ref[i]
        around = jnp.concatenate([edge, here[: lat - 1]], axis=0) + jnp.concatenate([here[1:], edge], axis=0)
        if i > 0:
            around += temp_ref[i - 1]
        if i < lon - 1:
            around += temp_ref[i + 1]
        base_ref[i] = here + DIFFUSION * (around - 4.0 * here) + heat_ref[i]


def shards(
    spectra, cloud_top, cloud_depth, sun_order, sunlit_cos, albedo, temp,
    extinction, scatter_albedo, gas_depth, band_map, solar_band, heat_factor,
):
    lon, lat, bins, levels = spectra.shape
    tall = -(-bins // 8) * 8
    rows = levels // 2 * PAIR * lat
    shape = jax.ShapeDtypeStruct((lon, lat, levels), jnp.float32)
    inputs = (
        jnp.transpose(spectra, (0, 2, 1, 3)), cloud_top, cloud_depth, sun_order, sunlit_cos, albedo,
        extinction, scatter_albedo, gas_depth, band_map[None], solar_band[None], heat_factor[None],
        cloud_top,
    )
    apart = [pl.BlockSpec(memory_space=pltpu.HBM)] * len(inputs)
    held = [pltpu.VMEM(x.shape, x.dtype) for x in inputs[:-1]] + [pltpu.SMEM(cloud_top.shape, cloud_top.dtype)]
    scratch = [
        pltpu.VMEM((tall * lat, levels), jnp.float32),
        pltpu.VMEM((rows, WIDE), jnp.float32),
        pltpu.VMEM((levels, WIDE), jnp.float32),
        pltpu.VMEM((tall, 2 * WIDE), jnp.bfloat16),
        pltpu.VMEM((rows, WIDE), jnp.float32),
        pltpu.VMEM((4, 8, WIDE), jnp.float32),
        pltpu.VMEM((rows, WIDE), jnp.float32),
        pltpu.VMEM((levels, WIDE), jnp.float32),
        pltpu.VMEM((2 * WIDE, levels), jnp.bfloat16),
        pltpu.VMEM((2 * WIDE, levels), jnp.bfloat16),
        pltpu.VMEM((2, PAIR * lat, WIDE), jnp.float32),
        pltpu.SemaphoreType.DMA((len(inputs),)),
    ]
    params = pltpu.CompilerParams(vmem_limit_bytes=60 * 1024 * 1024)
    early = pl.pallas_call(
        ahead_kernel,
        out_shape=shape,
        in_specs=apart,
        out_specs=pl.BlockSpec(memory_space=pltpu.HBM),
        scratch_shapes=held + [pltpu.VMEM(shape.shape, shape.dtype)] + scratch,
        compiler_params=params,
        name="radiation_ahead",
    )(*inputs)
    sent, early = lax.optimization_barrier((temp, early))

    def swap(axis, odd):
        n = lax.axis_size(axis)
        partner = [(i ^ 1) if odd == 0 else ((i + 1) % n if i % 2 else (i - 1) % n) for i in range(n)]
        return lax.ppermute(sent, axis, list(enumerate(partner)))

    col_a, col_b, gpt_a, gpt_b = swap("col", 0), swap("col", 1), swap("gpt", 0), swap("gpt", 1)
    heating, base = pl.pallas_call(
        after_kernel,
        out_shape=[shape, shape],
        in_specs=apart[:2] + apart,
        scratch_shapes=held
        + scratch[:-1]
        + [pltpu.VMEM(shape.shape, shape.dtype), pltpu.SemaphoreType.DMA((2,)), scratch[-1]],
        compiler_params=params,
        cost_estimate=pl.CostEstimate(flops=200_000_000, bytes_accessed=1 << 20, transcendentals=0),
        name="radiation_after",
    )(temp, early, *inputs)
    gpt_a, col_b, col_a, gpt_b = lax.optimization_barrier((gpt_a, col_b, col_a, gpt_b))
    base = lax.optimization_barrier(base)
    col_even = lax.rem(lax.axis_index("col"), 2) == 0
    gpt_even = lax.rem(lax.axis_index("gpt"), 2) == 0
    west = jnp.where(col_even, col_b[lon - 1 :], col_a[lon - 1 :])
    east = jnp.where(col_even, col_a[:1], col_b[:1])
    south = jnp.where(gpt_even, gpt_b[:, lat - 1 :], gpt_a[:, lat - 1 :])
    north = jnp.where(gpt_even, gpt_a[:, :1], gpt_b[:, :1])
    temp_next = base + DIFFUSION * (
        jnp.pad(west, ((0, lon - 1), (0, 0), (0, 0)))
        + jnp.pad(east, ((lon - 1, 0), (0, 0), (0, 0)))
        + jnp.pad(south, ((0, 0), (0, lat - 1), (0, 0)))
        + jnp.pad(north, ((0, 0), (lat - 1, 0), (0, 0)))
    )
    return (heating, temp_next)


def solution(mesh):
    column = P("col", "gpt")
    deep = P("col", "gpt", None)
    in_specs = (P("col", "gpt", None, None), column, column, column, column, deep, deep) + (P(),) * 6
    return jax.shard_map(shards, mesh=mesh, in_specs=in_specs, out_specs=(deep, deep), check_vma=False)
```

```python
import jax
import jax.numpy as jnp
from jax import lax
from jax.experimental import pallas as pl
from jax.experimental.pallas import tpu as pltpu
from jax.sharding import PartitionSpec as P

DIFFUSION = 0.2
CHUNK = 8
PAIR = 2
INPUTS = 13
PLAN = (352671002, 419779914, 1028, 1033, 1, 5, 0, 0)
WIDE = 128


def column_of(row, size):
    spread = jnp.broadcast_to(row, (size, size))
    lane = lax.broadcasted_iota(jnp.int32, (size, size), 1)
    sublane = lax.broadcasted_iota(jnp.int32, (size, size), 0)
    return jnp.sum(jnp.where(lane == sublane, spread, jnp.zeros_like(spread)), axis=1, keepdims=True)


def radiate(
    spectra, first, last,
    spec_ref, top_ref, depth_ref, order_ref, cos_ref, albedo_ref,
    ext_ref, scat_ref, gas_ref, band_ref, solar_ref, factor_ref, top_scalars,
    heat_ref,
    binned, rows_ref, gas_levels, table, steps, flat, gas_window, e_levels, clear_high, clear_low, ends,
):
    lon, bins, lat, levels = spec_ref.shape
    gpoints = ext_ref.shape[1]
    bands = albedo_ref.shape[2]
    tall = binned.shape[0] // lat
    group = PAIR * lat
    window = levels // 2

    table[...] = jnp.zeros_like(table)
    ext = ext_ref[...]
    table[:bins, :gpoints] = ext
    table[:bins, WIDE : WIDE + gpoints] = (ext.astype(jnp.float32) * scat_ref[...]).astype(jnp.bfloat16)

    gas = jnp.pad(gas_ref[...], ((0, WIDE - gpoints), (0, 0)))
    under = lax.broadcasted_iota(jnp.int32, (levels, levels), 0) > lax.broadcasted_iota(jnp.int32, (levels, levels), 1)
    below = jnp.dot(
        gas, under.astype(jnp.float32), precision=lax.Precision.HIGHEST, preferred_element_type=jnp.float32
    )
    t = 2.0 * gas
    rise = t * (1.0 + t * (0.5 + t * (1.0 / 6.0 + t * (1.0 / 24.0))))
    growth_below = jnp.exp(2.0 * below)
    growth = growth_below * (1.0 + rise)
    gas_levels[...] = gas.T
    e_levels[...] = growth.T
    for n, part in enumerate((growth_below * rise, rise / growth)):
        high = part.astype(jnp.bfloat16)
        clear_high[n * WIDE : (n + 1) * WIDE, :] = high
        clear_low[n * WIDE : (n + 1) * WIDE, :] = (part - high.astype(jnp.float32)).astype(jnp.bfloat16)

    onehot = (
        lax.broadcasted_iota(jnp.int32, (bands, gpoints), 0) == band_ref[...]
    ).astype(jnp.float32)
    solar_g = jnp.dot(
        solar_ref[...], onehot, precision=lax.Precision.HIGHEST, preferred_element_type=jnp.float32
    )
    onehot = onehot.astype(jnp.bfloat16)
    lev = lax.broadcasted_iota(jnp.int32, (lat, levels), 1).astype(jnp.float32)
    top = top_ref[...].astype(jnp.float32)
    flat[0, :lon, :lat] = top
    flat[1, :lon, :lat] = top + depth_ref[...].astype(jnp.float32)
    flat[2, :lon, :lat] = order_ref[...].astype(jnp.float32)
    flat[3, :lon, :lat] = cos_ref[...].astype(jnp.float32)
    binned[bins * lat :, :] = jnp.zeros((binned.shape[0] - bins * lat, levels), jnp.float32)

    spectra.wait()

    def one_pair(pair, nothing):
        surface, incoming, tops = [], [], []
        for i in range(PAIR):
            at_lon = pair * PAIR + i
            top, end, order, cosine = (column_of(flat[n, pl.ds(at_lon, 1), :lat], lat) for n in range(4))
            cloudy = ((lev >= top) & (lev < end)).astype(jnp.float32)
            for b in range(bins):
                binned[b * lat : (b + 1) * lat, :] = spec_ref[at_lon, b].astype(jnp.float32) * cloudy
            for j in range(lat):
                c = i * lat + j
                start = top_scalars[at_lon, j]
                column = pltpu.roll(binned[pl.ds(j, tall, stride=lat), :], lax.rem(levels - start, levels), 1)
                rows_ref[pl.ds(i * window * lat + j, window, stride=lat), :tall] = column.T[:window]
                gas_window[pl.ds(i * window * lat + j, window, stride=lat), :] = gas_levels[pl.ds(start, window), :]
                ends[0, c : c + 1, :] = e_levels[pl.ds(start, 1), :]
                ends[1, c : c + 1, :] = e_levels[pl.ds(start + window, 1), :]
            surf = jnp.dot(albedo_ref[at_lon], onehot, preferred_element_type=jnp.float32)
            lit = (order >= 0.0).astype(jnp.float32)
            surface.append(jnp.pad(surf, ((0, 0), (0, WIDE - gpoints))))
            incoming.append(jnp.pad((cosine * lit) * solar_g, ((0, 0), (0, WIDE - gpoints))))
            tops.append(top)

        begin = []
        for i in range(PAIR):
            e_end = ends[1, i * lat : (i + 1) * lat, :]
            upward = surface[i] / e_end
            begin.append((e_end - upward, e_end + upward))
        state = begin
        part = CHUNK * lat
        for chunk in reversed(range(window // CHUNK)):
            optics = []
            for i in range(PAIR):
                at = i * window * lat + chunk * part
                lhs = rows_ref[at : at + part, :tall].astype(jnp.bfloat16)
                both_kinds = jnp.dot(lhs, table[...], preferred_element_type=jnp.float32)
                optics.append(both_kinds.astype(jnp.bfloat16).astype(jnp.float32))
            for step in reversed(range(CHUNK)):
                for i in range(PAIR):
                    at = i * window * lat + (chunk * CHUNK + step) * lat
                    ext = optics[i][step * lat : (step + 1) * lat, :WIDE]
                    sca = optics[i][step * lat : (step + 1) * lat, WIDE:]
                    net, both = state[i]
                    total = ext + gas_window[at : at + lat, :]
                    a = total - sca
                    b = total - 0.85 * sca
                    p = a * b
                    grow = p * (2.0 + p * (2.0 / 3.0 + p * (4.0 / 45.0)))
                    slope = 2.0 + p * (4.0 / 3.0 + p * (4.0 / 15.0 + p * (8.0 / 315.0)))
                    d_net = grow * net + (a * slope) * both
                    d_both = grow * both + (b * slope) * net
                    steps[at : at + lat, :] = d_net
                    state[i] = (net + d_net, both + d_both)
        final = state

        weights, clear = [], []
        for i, (net, both) in enumerate(final):
            e_top = ends[0, i * lat : (i + 1) * lat, :]
            over = incoming[i] / e_levels[:1, :]
            weight = 2.0 * over * e_top / (net + both)
            weights.append(weight)
            clear.append(jnp.concatenate([over, 0.5 * weight * (both - net) * e_top], axis=1))
            clear.append(jnp.concatenate([weight, weight * surface[i]], axis=1))
        clear = jnp.concatenate(clear, axis=0)
        high = clear.astype(jnp.bfloat16)
        low = (clear - high.astype(jnp.float32)).astype(jnp.bfloat16)
        outside = (
            jnp.dot(high, clear_high[...], preferred_element_type=jnp.float32)
            + jnp.dot(high, clear_low[...], preferred_element_type=jnp.float32)
            + jnp.dot(low, clear_high[...], preferred_element_type=jnp.float32)
        )

        for i in range(PAIR):
            place = lev - tops[i]
            sums = jnp.where(place < 0.0, outside[2 * i * lat : (2 * i + 1) * lat],
                             outside[(2 * i + 1) * lat : (2 * i + 2) * lat])
            for k in range(window):
                part = steps[(i * window + k) * lat : (i * window + k + 1) * lat, :] * weights[i]
                sums = jnp.where(place == float(k), jnp.sum(part, axis=1, keepdims=True), sums)
            heat_ref[pair * PAIR + i] = sums * factor_ref[...]
        return nothing

    lax.fori_loop(first, last, one_pair, 0)


def pairs_ahead():
    at_col, at_gpt = lax.axis_index("col"), lax.axis_index("gpt")
    plan = jnp.where(at_gpt == 0, PLAN[0], jnp.where(at_gpt == 1, PLAN[1], jnp.where(at_gpt == 2, PLAN[2], PLAN[3])))
    high = jnp.where(at_gpt == 4, PLAN[4], jnp.where(at_gpt == 5, PLAN[5], jnp.where(at_gpt == 6, PLAN[6], PLAN[7])))
    return lax.shift_right_logical(jnp.where(at_gpt < 4, plan, high), 2 * at_col) & 3


def fetch(sources, held, arrived):
    copies = [pltpu.make_async_copy(s, h, arrived.at[n]) for n, (s, h) in enumerate(zip(sources, held))]
    for copy in copies:
        copy.start()
    for copy in copies[1:]:
        copy.wait()
    return copies[0]


def ahead_kernel(*refs):
    count = INPUTS
    sources, out_ref = refs[:count], refs[count]
    held, heat_ref = refs[count + 1 : 2 * count + 1], refs[2 * count + 1]
    scratch, arrived = refs[2 * count + 2 : -1], refs[-1]
    pairs = pairs_ahead()

    @pl.when(pairs > 0)
    def _():
        spectra = fetch(sources, held, arrived)
        radiate(spectra, 0, pairs, *held, heat_ref, *scratch)
        leave = pltpu.make_async_copy(heat_ref, out_ref, arrived.at[0])
        leave.start()
        leave.wait()


def after_kernel(temp_ref, early_ref, *refs):
    count = INPUTS
    sources, (heat_ref, base_ref) = refs[:count], refs[count : count + 2]
    held, scratch = refs[count + 2 : 2 * count + 2], refs[2 * count + 2 : -3]
    own_ref, two, arrived = refs[-3:]
    lon, lat, levels = temp_ref.shape
    pairs = pairs_ahead()
    early = pltpu.make_async_copy(early_ref, heat_ref, two.at[0])
    early.start()
    own = pltpu.make_async_copy(temp_ref, own_ref, two.at[1])
    own.start()

    @pl.when(pairs < lon // PAIR)
    def _():
        spectra = fetch(sources, held, arrived)
        early.wait()
        radiate(spectra, pairs, lon // PAIR, *held, heat_ref, *scratch)

    @pl.when(pairs == lon // PAIR)
    def _():
        early.wait()

    own.wait()
    temp_ref = own_ref
    edge = jnp.zeros((1, levels), jnp.float32)
    for i in range(lon):
        here = temp_ref[i]
        around = jnp.concatenate([edge, here[: lat - 1]], axis=0) + jnp.concatenate([here[1:], edge], axis=0)
        if i > 0:
            around += temp_ref[i - 1]
        if i < lon - 1:
            around += temp_ref[i + 1]
        base_ref[i] = here + DIFFUSION * (around - 4.0 * here) + heat_ref[i]


def shards(
    spectra, cloud_top, cloud_depth, sun_order, sunlit_cos, albedo, temp,
    extinction, scatter_albedo, gas_depth, band_map, solar_band, heat_factor,
):
    lon, lat, bins, levels = spectra.shape
    tall = -(-bins // 8) * 8
    rows = levels // 2 * PAIR * lat
    shape = jax.ShapeDtypeStruct((lon, lat, levels), jnp.float32)
    inputs = (
        jnp.transpose(spectra, (0, 2, 1, 3)), cloud_top, cloud_depth, sun_order, sunlit_cos, albedo,
        extinction, scatter_albedo, gas_depth, band_map[None], solar_band[None], heat_factor[None],
        cloud_top,
    )
    apart = [pl.BlockSpec(memory_space=pltpu.HBM)] * len(inputs)
    held = [pltpu.VMEM(x.shape, x.dtype) for x in inputs[:-1]] + [pltpu.SMEM(cloud_top.shape, cloud_top.dtype)]
    scratch = [
        pltpu.VMEM((tall * lat, levels), jnp.float32),
        pltpu.VMEM((rows, WIDE), jnp.float32),
        pltpu.VMEM((levels, WIDE), jnp.float32),
        pltpu.VMEM((tall, 2 * WIDE), jnp.bfloat16),
        pltpu.VMEM((rows, WIDE), jnp.float32),
        pltpu.VMEM((4, 8, WIDE), jnp.float32),
        pltpu.VMEM((rows, WIDE), jnp.float32),
        pltpu.VMEM((levels, WIDE), jnp.float32),
        pltpu.VMEM((2 * WIDE, levels), jnp.bfloat16),
        pltpu.VMEM((2 * WIDE, levels), jnp.bfloat16),
        pltpu.VMEM((2, PAIR * lat, WIDE), jnp.float32),
        pltpu.SemaphoreType.DMA((len(inputs),)),
    ]
    params = pltpu.CompilerParams(vmem_limit_bytes=60 * 1024 * 1024)
    early = pl.pallas_call(
        ahead_kernel,
        out_shape=shape,
        in_specs=apart,
        out_specs=pl.BlockSpec(memory_space=pltpu.HBM),
        scratch_shapes=held + [pltpu.VMEM(shape.shape, shape.dtype)] + scratch,
        compiler_params=params,
        name="radiation_ahead",
    )(*inputs)
    sent, early = lax.optimization_barrier((temp, early))

    def swap(axis, odd):
        n = lax.axis_size(axis)
        partner = [(i ^ 1) if odd == 0 else ((i + 1) % n if i % 2 else (i - 1) % n) for i in range(n)]
        return lax.ppermute(sent, axis, list(enumerate(partner)))

    col_a, col_b, gpt_a, gpt_b = swap("col", 0), swap("col", 1), swap("gpt", 0), swap("gpt", 1)
    heating, base = pl.pallas_call(
        after_kernel,
        out_shape=[shape, shape],
        in_specs=apart[:2] + apart,
        scratch_shapes=held
        + scratch[:-1]
        + [pltpu.VMEM(shape.shape, shape.dtype), pltpu.SemaphoreType.DMA((2,)), scratch[-1]],
        compiler_params=params,
        cost_estimate=pl.CostEstimate(flops=200_000_000, bytes_accessed=1 << 20, transcendentals=0),
        name="radiation_after",
    )(temp, early, *inputs)
    gpt_a, col_b, col_a, gpt_b = lax.optimization_barrier((gpt_a, col_b, col_a, gpt_b))
    base = lax.optimization_barrier(base)
    col_even = lax.rem(lax.axis_index("col"), 2) == 0
    gpt_even = lax.rem(lax.axis_index("gpt"), 2) == 0
    west = jnp.where(col_even, col_b[lon - 1 :], col_a[lon - 1 :])
    east = jnp.where(col_even, col_a[:1], col_b[:1])
    south = jnp.where(gpt_even, gpt_b[:, lat - 1 :], gpt_a[:, lat - 1 :])
    north = jnp.where(gpt_even, gpt_a[:, :1], gpt_b[:, :1])
    temp_next = base + DIFFUSION * (
        jnp.pad(west, ((0, lon - 1), (0, 0), (0, 0)))
        + jnp.pad(east, ((lon - 1, 0), (0, 0), (0, 0)))
        + jnp.pad(south, ((0, 0), (0, lat - 1), (0, 0)))
        + jnp.pad(north, ((0, 0), (lat - 1, 0), (0, 0)))
    )
    return (heating, temp_next)


def solution(mesh):
    column = P("col", "gpt")
    deep = P("col", "gpt", None)
    in_specs = (P("col", "gpt", None, None), column, column, column, column, deep, deep) + (P(),) * 6
    return jax.shard_map(shards, mesh=mesh, in_specs=in_specs, out_specs=(deep, deep), check_vma=False)
```

```python
import jax
import jax.numpy as jnp
from jax import lax
from jax.experimental import pallas as pl
from jax.experimental.pallas import tpu as pltpu
from jax.sharding import PartitionSpec as P

DIFFUSION = 0.2
CHUNK = 8
PAIR = 2
INPUTS = 13
PLAN = (352671002, 419779914, 1028, 1033, 1, 5, 0, 0)
WIDE = 128


def column_of(row, size):
    spread = jnp.broadcast_to(row, (size, size))
    lane = lax.broadcasted_iota(jnp.int32, (size, size), 1)
    sublane = lax.broadcasted_iota(jnp.int32, (size, size), 0)
    return jnp.sum(jnp.where(lane == sublane, spread, jnp.zeros_like(spread)), axis=1, keepdims=True)


def radiate(
    spectra, first, last,
    spec_ref, top_ref, depth_ref, order_ref, cos_ref, albedo_ref,
    ext_ref, scat_ref, gas_ref, band_ref, solar_ref, factor_ref, top_scalars,
    heat_ref,
    binned, rows_ref, gas_levels, table, steps, flat, gas_window, e_levels, clear_high, clear_low, ends,
):
    lon, bins, lat, levels = spec_ref.shape
    gpoints = ext_ref.shape[1]
    bands = albedo_ref.shape[2]
    tall = binned.shape[0] // lat
    group = PAIR * lat
    window = levels // 2

    table[...] = jnp.zeros_like(table)
    ext = ext_ref[...]
    table[:bins, :gpoints] = ext
    table[:bins, WIDE : WIDE + gpoints] = (ext.astype(jnp.float32) * scat_ref[...]).astype(jnp.bfloat16)

    gas = jnp.pad(gas_ref[...], ((0, WIDE - gpoints), (0, 0)))
    under = lax.broadcasted_iota(jnp.int32, (levels, levels), 0) > lax.broadcasted_iota(jnp.int32, (levels, levels), 1)
    under = under.astype(jnp.float32).astype(jnp.bfloat16)
    below, left = jnp.zeros((WIDE, levels), jnp.float32), gas
    for _ in range(3):
        piece = left.astype(jnp.bfloat16)
        below += jnp.dot(piece, under, preferred_element_type=jnp.float32)
        left = left - piece.astype(jnp.float32)
    t = 2.0 * gas
    rise = t * (1.0 + t * (0.5 + t * (1.0 / 6.0 + t * (1.0 / 24.0))))
    growth_below = jnp.exp(2.0 * below)
    growth = growth_below * (1.0 + rise)
    gas_levels[...] = gas.T
    e_levels[...] = growth.T
    for n, part in enumerate((growth_below * rise, rise / growth)):
        high = part.astype(jnp.bfloat16)
        clear_high[n * WIDE : (n + 1) * WIDE, :] = high
        clear_low[n * WIDE : (n + 1) * WIDE, :] = (part - high.astype(jnp.float32)).astype(jnp.bfloat16)

    onehot = (
        lax.broadcasted_iota(jnp.int32, (bands, gpoints), 0) == band_ref[...]
    ).astype(jnp.float32)
    solar_g = jnp.sum(onehot * column_of(solar_ref[...], bands), axis=0, keepdims=True)
    onehot = onehot.astype(jnp.bfloat16)
    lev = lax.broadcasted_iota(jnp.int32, (lat, levels), 1).astype(jnp.float32)
    top = top_ref[...].astype(jnp.float32)
    flat[0, :lon, :lat] = top
    flat[1, :lon, :lat] = top + depth_ref[...].astype(jnp.float32)
    flat[2, :lon, :lat] = order_ref[...].astype(jnp.float32)
    flat[3, :lon, :lat] = cos_ref[...].astype(jnp.float32)
    binned[bins * lat :, :] = jnp.zeros((binned.shape[0] - bins * lat, levels), jnp.float32)

    spectra.wait()

    def one_pair(pair, nothing):
        surface, incoming, tops = [], [], []
        for i in range(PAIR):
            at_lon = pair * PAIR + i
            top, end, order, cosine = (column_of(flat[n, pl.ds(at_lon, 1), :lat], lat) for n in range(4))
            cloudy = ((lev >= top) & (lev < end)).astype(jnp.float32)
            for b in range(bins):
                binned[b * lat : (b + 1) * lat, :] = spec_ref[at_lon, b].astype(jnp.float32) * cloudy
            for j in range(lat):
                c = i * lat + j
                start = top_scalars[at_lon, j]
                column = pltpu.roll(binned[pl.ds(j, tall, stride=lat), :], lax.rem(levels - start, levels), 1)
                rows_ref[pl.ds(i * window * lat + j, window, stride=lat), :tall] = column.T[:window]
                gas_window[pl.ds(i * window * lat + j, window, stride=lat), :] = gas_levels[pl.ds(start, window), :]
                ends[0, c : c + 1, :] = e_levels[pl.ds(start, 1), :]
                ends[1, c : c + 1, :] = e_levels[pl.ds(start + window, 1), :]
            surf = jnp.dot(albedo_ref[at_lon], onehot, preferred_element_type=jnp.float32)
            lit = (order >= 0.0).astype(jnp.float32)
            surface.append(jnp.pad(surf, ((0, 0), (0, WIDE - gpoints))))
            incoming.append(jnp.pad((cosine * lit) * solar_g, ((0, 0), (0, WIDE - gpoints))))
            tops.append(top)

        begin = []
        for i in range(PAIR):
            e_end = ends[1, i * lat : (i + 1) * lat, :]
            upward = surface[i] / e_end
            begin.append((e_end - upward, e_end + upward))
        state = begin
        part = CHUNK * lat
        for chunk in reversed(range(window // CHUNK)):
            optics = []
            for i in range(PAIR):
                at = i * window * lat + chunk * part
                lhs = rows_ref[at : at + part, :tall].astype(jnp.bfloat16)
                both_kinds = jnp.dot(lhs, table[...], preferred_element_type=jnp.float32)
                optics.append(both_kinds.astype(jnp.bfloat16).astype(jnp.float32))
            for step in reversed(range(CHUNK)):
                for i in range(PAIR):
                    at = i * window * lat + (chunk * CHUNK + step) * lat
                    ext = optics[i][step * lat : (step + 1) * lat, :WIDE]
                    sca = optics[i][step * lat : (step + 1) * lat, WIDE:]
                    net, both = state[i]
                    total = ext + gas_window[at : at + lat, :]
                    a = total - sca
                    b = total - 0.85 * sca
                    p = a * b
                    grow = p * (2.0 + p * (2.0 / 3.0 + p * (4.0 / 45.0)))
                    slope = 2.0 + p * (4.0 / 3.0 + p * (4.0 / 15.0 + p * (8.0 / 315.0)))
                    d_net = grow * net + (a * slope) * both
                    d_both = grow * both + (b * slope) * net
                    steps[at : at + lat, :] = d_net
                    state[i] = (net + d_net, both + d_both)
        final = state

        weights, clear = [], []
        for i, (net, both) in enumerate(final):
            e_top = ends[0, i * lat : (i + 1) * lat, :]
            over = incoming[i] / e_levels[:1, :]
            weight = 2.0 * over * e_top / (net + both)
            weights.append(weight)
            clear.append(jnp.concatenate([over, 0.5 * weight * (both - net) * e_top], axis=1))
            clear.append(jnp.concatenate([weight, weight * surface[i]], axis=1))
        clear = jnp.concatenate(clear, axis=0)
        high = clear.astype(jnp.bfloat16)
        low = (clear - high.astype(jnp.float32)).astype(jnp.bfloat16)
        outside = (
            jnp.dot(high, clear_high[...], preferred_element_type=jnp.float32)
            + jnp.dot(high, clear_low[...], preferred_element_type=jnp.float32)
            + jnp.dot(low, clear_high[...], preferred_element_type=jnp.float32)
        )

        for i in range(PAIR):
            place = lev - tops[i]
            sums = jnp.where(place < 0.0, outside[2 * i * lat : (2 * i + 1) * lat],
                             outside[(2 * i + 1) * lat : (2 * i + 2) * lat])
            for k in range(window):
                part = steps[(i * window + k) * lat : (i * window + k + 1) * lat, :] * weights[i]
                sums = jnp.where(place == float(k), jnp.sum(part, axis=1, keepdims=True), sums)
            heat_ref[pair * PAIR + i] = sums * factor_ref[...]
        return nothing

    lax.fori_loop(first, last, one_pair, 0)


def pairs_ahead():
    at_col, at_gpt = lax.axis_index("col"), lax.axis_index("gpt")
    plan = jnp.where(at_gpt == 0, PLAN[0], jnp.where(at_gpt == 1, PLAN[1], jnp.where(at_gpt == 2, PLAN[2], PLAN[3])))
    high = jnp.where(at_gpt == 4, PLAN[4], jnp.where(at_gpt == 5, PLAN[5], jnp.where(at_gpt == 6, PLAN[6], PLAN[7])))
    return lax.shift_right_logical(jnp.where(at_gpt < 4, plan, high), 2 * at_col) & 3


def fetch(sources, held, arrived):
    copies = [pltpu.make_async_copy(s, h, arrived.at[n]) for n, (s, h) in enumerate(zip(sources, held))]
    for copy in copies:
        copy.start()
    for copy in copies[1:]:
        copy.wait()
    return copies[0]


def ahead_kernel(*refs):
    count = INPUTS
    sources, out_ref = refs[:count], refs[count]
    held, heat_ref = refs[count + 1 : 2 * count + 1], refs[2 * count + 1]
    scratch, arrived = refs[2 * count + 2 : -1], refs[-1]
    pairs = pairs_ahead()

    @pl.when(pairs > 0)
    def _():
        spectra = fetch(sources, held, arrived)
        radiate(spectra, 0, pairs, *held, heat_ref, *scratch)
        leave = pltpu.make_async_copy(heat_ref, out_ref, arrived.at[0])
        leave.start()
        leave.wait()


def after_kernel(temp_ref, early_ref, *refs):
    count = INPUTS
    sources, (heat_ref, base_ref) = refs[:count], refs[count : count + 2]
    held, scratch = refs[count + 2 : 2 * count + 2], refs[2 * count + 2 : -3]
    own_ref, two, arrived = refs[-3:]
    lon, lat, levels = temp_ref.shape
    pairs = pairs_ahead()
    early = pltpu.make_async_copy(early_ref, heat_ref, two.at[0])
    early.start()
    own = pltpu.make_async_copy(temp_ref, own_ref, two.at[1])
    own.start()

    @pl.when(pairs < lon // PAIR)
    def _():
        spectra = fetch(sources, held, arrived)
        early.wait()
        radiate(spectra, pairs, lon // PAIR, *held, heat_ref, *scratch)

    @pl.when(pairs == lon // PAIR)
    def _():
        early.wait()

    own.wait()
    temp_ref = own_ref
    edge = jnp.zeros((1, levels), jnp.float32)
    for i in range(lon):
        here = temp_ref[i]
        around = jnp.concatenate([edge, here[: lat - 1]], axis=0) + jnp.concatenate([here[1:], edge], axis=0)
        if i > 0:
            around += temp_ref[i - 1]
        if i < lon - 1:
            around += temp_ref[i + 1]
        base_ref[i] = here + DIFFUSION * (around - 4.0 * here) + heat_ref[i]


def shards(
    spectra, cloud_top, cloud_depth, sun_order, sunlit_cos, albedo, temp,
    extinction, scatter_albedo, gas_depth, band_map, solar_band, heat_factor,
):
    lon, lat, bins, levels = spectra.shape
    tall = -(-bins // 8) * 8
    rows = levels // 2 * PAIR * lat
    shape = jax.ShapeDtypeStruct((lon, lat, levels), jnp.float32)
    inputs = (
        jnp.transpose(spectra, (0, 2, 1, 3)), cloud_top, cloud_depth, sun_order, sunlit_cos, albedo,
        extinction, scatter_albedo, gas_depth, band_map[None], solar_band[None], heat_factor[None],
        cloud_top,
    )
    apart = [pl.BlockSpec(memory_space=pltpu.HBM)] * len(inputs)
    held = [pltpu.VMEM(x.shape, x.dtype) for x in inputs[:-1]] + [pltpu.SMEM(cloud_top.shape, cloud_top.dtype)]
    scratch = [
        pltpu.VMEM((tall * lat, levels), jnp.float32),
        pltpu.VMEM((rows, WIDE), jnp.float32),
        pltpu.VMEM((levels, WIDE), jnp.float32),
        pltpu.VMEM((tall, 2 * WIDE), jnp.bfloat16),
        pltpu.VMEM((rows, WIDE), jnp.float32),
        pltpu.VMEM((4, 8, WIDE), jnp.float32),
        pltpu.VMEM((rows, WIDE), jnp.float32),
        pltpu.VMEM((levels, WIDE), jnp.float32),
        pltpu.VMEM((2 * WIDE, levels), jnp.bfloat16),
        pltpu.VMEM((2 * WIDE, levels), jnp.bfloat16),
        pltpu.VMEM((2, PAIR * lat, WIDE), jnp.float32),
        pltpu.SemaphoreType.DMA((len(inputs),)),
    ]
    params = pltpu.CompilerParams(vmem_limit_bytes=60 * 1024 * 1024)
    early = pl.pallas_call(
        ahead_kernel,
        out_shape=shape,
        in_specs=apart,
        out_specs=pl.BlockSpec(memory_space=pltpu.HBM),
        scratch_shapes=held + [pltpu.VMEM(shape.shape, shape.dtype)] + scratch,
        compiler_params=params,
        name="radiation_ahead",
    )(*inputs)
    sent, early = lax.optimization_barrier((temp, early))

    def swap(axis, odd):
        n = lax.axis_size(axis)
        partner = [(i ^ 1) if odd == 0 else ((i + 1) % n if i % 2 else (i - 1) % n) for i in range(n)]
        return lax.ppermute(sent, axis, list(enumerate(partner)))

    col_a, col_b, gpt_a, gpt_b = swap("col", 0), swap("col", 1), swap("gpt", 0), swap("gpt", 1)
    heating, base = pl.pallas_call(
        after_kernel,
        out_shape=[shape, shape],
        in_specs=apart[:2] + apart,
        scratch_shapes=held
        + scratch[:-1]
        + [pltpu.VMEM(shape.shape, shape.dtype), pltpu.SemaphoreType.DMA((2,)), scratch[-1]],
        compiler_params=params,
        cost_estimate=pl.CostEstimate(flops=200_000_000, bytes_accessed=1 << 20, transcendentals=0),
        name="radiation_after",
    )(temp, early, *inputs)
    gpt_a, col_b, col_a, gpt_b = lax.optimization_barrier((gpt_a, col_b, col_a, gpt_b))
    base = lax.optimization_barrier(base)
    col_even = lax.rem(lax.axis_index("col"), 2) == 0
    gpt_even = lax.rem(lax.axis_index("gpt"), 2) == 0
    west = jnp.where(col_even, col_b[lon - 1 :], col_a[lon - 1 :])
    east = jnp.where(col_even, col_a[:1], col_b[:1])
    south = jnp.where(gpt_even, gpt_b[:, lat - 1 :], gpt_a[:, lat - 1 :])
    north = jnp.where(gpt_even, gpt_a[:, :1], gpt_b[:, :1])
    temp_next = base + DIFFUSION * (
        jnp.pad(west, ((0, lon - 1), (0, 0), (0, 0)))
        + jnp.pad(east, ((lon - 1, 0), (0, 0), (0, 0)))
        + jnp.pad(south, ((0, 0), (0, lat - 1), (0, 0)))
        + jnp.pad(north, ((0, 0), (lat - 1, 0), (0, 0)))
    )
    return (heating, temp_next)


def solution(mesh):
    column = P("col", "gpt")
    deep = P("col", "gpt", None)
    in_specs = (P("col", "gpt", None, None), column, column, column, column, deep, deep) + (P(),) * 6
    return jax.shard_map(shards, mesh=mesh, in_specs=in_specs, out_specs=(deep, deep), check_vma=False)
```
